32 devices in a mesh: shard: 8 (over z, y), blk: 4 (over x, core).
Axes of the slice: x: 2, y: 2, z: 4, core: 2. Of those that a mesh axis runs over, the one named last changes fastest.
Arguments:
- request_embeddings: bfloat16 [8192, 256], P(('shard', 'blk')), may hold values from -0.5 to 0.5
- frequent_entry_matrix: bfloat16 [2048, 256], replicated, may hold values from -0.23925781 to 0.23925781
- rare_entry_matrix: float32 [16384, 256], P('shard'), may hold values from -0.24 to 0.24
- frequent_entry_lines: int32 [8192, 4], P(('shard', 'blk')), may hold values from 0 to 2047
- rare_place_parent: int32 [8192, 4], P(('shard', 'blk')), may hold values from 0 to 7, all different within a row; in each aligned block of 256 rows (0 to 255, 256 to 511, ...) at most 256 rows name the same one
- rare_local_position: int32 [8192, 4], P(('shard', 'blk')), may hold values from 0 to 2047
- rare_place_tally: int32 [8192], P(('shard', 'blk')), may hold values from 1 to 4
- sharpness_factor: float32 [1], replicated, may hold values from 4 to 16
- pairscore_additive: float32 [1], replicated, may hold values from -6 to -2
Outputs:
- request_derivative: float32 [8192, 256], P(('shard', 'blk'))
- hot_grad: float32 [2048, 256], replicated
- cold_grad: float32 [16384, 256], P(('shard', 'blk'))
The draws below stay inside these ranges and needn't reach their ends.
Inputs may be any that keep to these rules, and one draw needn't show every extreme that they name: `rare_place_parent`: each row names 4 different owners; among the rows of one device no owner is named by more than 256 rows, a bound that some block reaches.
All inputs are finite; a program needn't handle non-finite values.
Results may differ from the reference program's by a relative error of at most 0.007.
Values may be sent and summed in bfloat16 or wider, within the bound.
A program may use at most 64 MiB of HBM per device.

```python
import math
import jax
import jax.numpy as jnp
import numpy as np
from jax import lax

E = 256
HB = 4
CB = 4
PAIRS = 256
HOT = 2048
COLD_DEV = 2048
CAP = 256
NP = 8192
COLD_ROWS = 16384
N_SHARD = 8
N_BLK = 4


def place_ends(entries, own_key, low, top_value):
    extent = entries.shape
    place = [jax.random.randint(jax.random.fold_in(own_key, axis), (), 0, extent[axis]) for axis in range(len(extent))]
    entries = entries.at[tuple(place)].set(low)
    longest = extent.index(max(extent))
    place[longest] = (place[longest] + 1) % extent[longest]
    return entries.at[tuple(place)].set(top_value)


def level_of(stream_key, shape, pieces, least, high):
    def one(dim, shards_of):
        draws = jax.random.uniform(jax.random.fold_in(jax.random.fold_in(stream_key, 6), dim), (shards_of,), jnp.float32, least / len(pieces), high / len(pieces))
        return jnp.repeat(jnp.exp(draws), shape[dim] // shards_of).reshape((-1,) + (1,) * (len(shape) - dim - 1))

    gain = one(*pieces[0])
    for cut in pieces[1:]:
        gain = gain * one(*cut)
    return gain


def cumulative_ranks(count, lean):
    portions = [(1 << 20) // math.isqrt(rank ** lean) + 1 for rank in range(1, count + 1)]
    spread = 1 + sum(portions) // (1 << 30)
    return np.cumsum(np.array([max(1, weight // spread) for weight in portions]))


def ranked_ids(own_key, dims, amount, slope):
    table = cumulative_ranks(amount, slope)
    ticket = jax.random.randint(jax.random.fold_in(own_key, 1), dims, 0, int(table[amount - 1]))
    standing = jnp.searchsorted(jnp.asarray(table, jnp.int32), ticket, side="right")
    return jax.random.permutation(jax.random.fold_in(own_key, 2), amount)[standing].astype(jnp.int32)


def routed_block(own_key, own, number, rows, count, top, most, slope):
    ranking = jax.random.permutation(own_key, count)
    packed, common = load_shares(count, rows * top, most, slope, True), load_shares(count, rows * top, most, slope, False)
    places = jnp.arange(count)

    def named(lengths, offset_by):
        used = int((lengths > 0).sum())
        fixed = max(1, used // 4)
        passed = fixed + (places - fixed + offset_by * (used - fixed)) % max(1, count - fixed)
        return jnp.zeros((count,), jnp.int32).at[ranking[jnp.where(places < fixed, places, passed)]].set(jnp.asarray(lengths, jnp.int32))

    lengths = jnp.where(number % 4 == 0, named(packed, number // 4), named(common, number - number // 4 - 1))
    mixed = jax.random.permutation(jax.random.fold_in(own, 3), count)
    giver, receiver = mixed[0:count // 2 * 2:2], mixed[1:count // 2 * 2:2]
    margin = jnp.minimum(lengths[giver] - 1, most - lengths[receiver]) // 2
    margin = jnp.where((giver == ranking[0]) | (receiver == ranking[0]) | (lengths[receiver] == 0), 0, jnp.maximum(margin, 0))
    passed = jax.random.randint(jax.random.fold_in(own, 4), (count // 2,), 0, 1 << 20) % (margin + 1)
    lengths = lengths.at[giver].add(-passed).at[receiver].add(passed)
    members = jnp.searchsorted(jnp.cumsum(lengths), jnp.arange(rows * top), side="right").astype(jnp.int32)
    listing = members.reshape(top, rows).T
    listing = listing[jax.random.permutation(jax.random.fold_in(own, 1), rows)]
    offset_by = jax.random.randint(jax.random.fold_in(own, 2), (rows, 1), 0, top)
    return jnp.take_along_axis(listing, (jnp.arange(top)[None, :] + offset_by) % top, axis=1)


def load_shares(count, total, limit, slope, full):
    portions = [(1 << 20) // math.isqrt(rank ** slope) + 1 for rank in range(1, count + 1)]
    largest = limit if full else min(limit, max(-(-total // count), total * portions[0] // sum(portions)))
    least = 1 if total - largest >= count - 1 else 0
    holding, rest = [largest] + [least] * (count - 1), total - largest - least * (count - 1)
    while rest > 0:
        free = [i for i in range(1, count) if holding[i] < largest] or [i for i in range(1, count) if holding[i] < limit]
        whole, left = sum([portions[i] for i in free]), rest
        for i in free:
            addition = min(limit - holding[i], max(1, left * portions[i] // whole), rest)
            holding[i] = holding[i] + addition
            rest = rest - addition
    return np.array(holding)


def scatter_about(stream_key, dims, deviation, limit, shards=(), held_as=jnp.bfloat16):
    values = jax.random.normal(stream_key, dims, jnp.float32) * deviation
    if len(shards) > 0:
        values = level_of(stream_key, dims, shards, -0.22, 0.18) * values
    return jnp.clip(values, min=-limit, max=limit).astype(held_as)


def setup_inputs(seed: int = 0) -> dict:
    streams_of = jax.random.split(jax.random.key(seed), 10)
    request_embeddings = scatter_about(streams_of[0], (NP, E), 0.0625, 0.5, ((0, 32),))
    frequent_entry_matrix = scatter_about(streams_of[1], (HOT, E), 0.03, 0.23925781)
    rare_entry_matrix = scatter_about(streams_of[2], (COLD_ROWS, E), 0.03, 0.24, ((0, 8),), jnp.float32)
    frequent_entry_lines = place_ends(ranked_ids(streams_of[3], (NP, HB), HOT, 1), jax.random.fold_in(streams_of[3], 3), 0, HOT - 1).astype(jnp.int32)
    rare_place_parent_keys = jax.random.split(jax.random.fold_in(streams_of[4], 1), NP // PAIRS)
    rare_place_parent_turns = jax.random.permutation(jax.random.fold_in(streams_of[4], 3), NP // PAIRS)
    rare_place_parent = jax.vmap(lambda own, number: routed_block(jax.random.fold_in(streams_of[4], 2), own, number, PAIRS, N_SHARD, CB, CAP, 2))(rare_place_parent_keys, rare_place_parent_turns).reshape((NP, CB))
    rare_local_position = place_ends(jax.random.randint(streams_of[5], (NP, CB), 0, COLD_DEV), jax.random.fold_in(streams_of[5], 1), 0, COLD_DEV - 1).astype(jnp.int32)
    rare_place_tally = place_ends(jax.random.randint(streams_of[6], (NP,), 1, CB + 1), jax.random.fold_in(streams_of[6], 1), 1, CB).astype(jnp.int32)
    sharpness_factor = jnp.clip(jnp.exp(jax.random.uniform(streams_of[7], (1,), jnp.float32, math.log(4.0), math.log(16.0))), 4.0, 16.0)
    pairscore_additive = jnp.clip(jax.random.uniform(streams_of[8], (1,), jnp.float32, -6.0, -2.0), -6.0, -2.0)
    return dict(request_embeddings=request_embeddings, frequent_entry_matrix=frequent_entry_matrix, rare_entry_matrix=rare_entry_matrix, frequent_entry_lines=frequent_entry_lines, rare_place_parent=rare_place_parent, rare_local_position=rare_local_position, rare_place_tally=rare_place_tally, sharpness_factor=sharpness_factor, pairscore_additive=pairscore_additive)


epsilon = 1e-06

def normalize_rows(vectors):
    radius = jnp.sqrt(lax.optimization_barrier(jnp.sum(vectors * vectors, axis=1, keepdims=True)) + epsilon)
    return (vectors / radius, radius)

def projection_backward(unit_vectors, radius, gradient):
    inner = lax.optimization_barrier(jnp.sum(unit_vectors * gradient, axis=1, keepdims=True))
    return (gradient - unit_vectors * inner) / radius

def reference(request_embeddings, frequent_entry_matrix, rare_entry_matrix, frequent_entry_lines, rare_place_parent, rare_local_position, rare_place_tally, sharpness_factor, pairscore_additive):
    group_size = PAIRS * N_BLK
    sharpness_multiplier = sharpness_factor[0]
    additive_term = pairscore_additive[0]
    slot_index = jnp.arange(CB, dtype=jnp.int32)
    diagonal = jnp.arange(group_size, dtype=jnp.int32)

    def one_group(running, group_index):
        hot_acc, cold_acc = running
        first_row = (group_index * group_size).astype(jnp.int32)
        features = lax.dynamic_slice_in_dim(request_embeddings, first_row, group_size, 0).astype(jnp.float32)
        hot_slots = lax.dynamic_slice_in_dim(frequent_entry_lines, first_row, group_size, 0)
        owners = lax.dynamic_slice_in_dim(rare_place_parent, first_row, group_size, 0)
        offsets = lax.dynamic_slice_in_dim(rare_local_position, first_row, group_size, 0)
        counts = lax.dynamic_slice_in_dim(rare_place_tally, first_row, group_size, 0)
        cold_rows = (owners * COLD_DEV + offsets).astype(jnp.int32)
        live_slot = (slot_index[None, :] < counts[:, None]).astype(jnp.float32)
        hot_sum = lax.optimization_barrier(jnp.sum(jnp.take(frequent_entry_matrix, hot_slots, axis=0).astype(jnp.float32), axis=1))
        cold_sum = lax.optimization_barrier(jnp.sum(jnp.take(rare_entry_matrix, cold_rows, axis=0) * live_slot[:, :, None], axis=1))
        candidate_normalized, candidate_norm = normalize_rows(hot_sum + cold_sum)
        request_normalized, request_norm = normalize_rows(features)
        candidate_reduced = candidate_normalized.astype(jnp.bfloat16)
        request_reduced = request_normalized.astype(jnp.bfloat16)
        pairwise_scores = sharpness_multiplier * lax.dot_general(request_reduced, candidate_reduced, (((1,), (1,)), ((), ())), preferred_element_type=jnp.float32) + additive_term
        positive = (diagonal[:, None] == diagonal[None, :]).astype(jnp.float32)
        pairscore_derivative = (jax.nn.sigmoid(pairwise_scores) - positive).astype(jnp.bfloat16)
        request_direction = sharpness_multiplier * jnp.dot(pairscore_derivative, candidate_reduced, preferred_element_type=jnp.float32)
        candidate_direction = sharpness_multiplier * lax.dot_general(pairscore_derivative, request_reduced, (((0,), (0,)), ((), ())), preferred_element_type=jnp.float32)
        request_derivative = projection_backward(request_normalized, request_norm, request_direction)
        item_low_grad = lax.optimization_barrier(projection_backward(candidate_normalized, candidate_norm, candidate_direction).astype(jnp.bfloat16))
        candidate_derivative = item_low_grad.astype(jnp.float32)
        hot_acc = hot_acc.at[hot_slots.reshape(-1)].add(jnp.repeat(candidate_derivative, HB, axis=0))
        cold_terms = jnp.repeat(candidate_derivative, CB, axis=0) * live_slot.reshape(-1)[:, None]
        cold_acc = cold_acc.at[cold_rows.reshape(-1)].add(cold_terms)
        return ((hot_acc, cold_acc), request_derivative)
    start_state = (jnp.zeros((HOT, E), jnp.float32), jnp.zeros((N_SHARD * COLD_DEV, E), jnp.float32))
    (hot_grad, cold_grad), query_parts = lax.scan(one_group, start_state, jnp.arange(N_SHARD, dtype=jnp.int32))
    return (query_parts.reshape(N_SHARD * group_size, E), hot_grad, cold_grad)
```

```python
import functools

import jax
import jax.numpy as jnp
from jax import lax
from jax.experimental import pallas as pl
from jax.experimental.pallas import tpu as pltpu
from jax.sharding import PartitionSpec as P

epsilon = 1e-06
BF = jnp.bfloat16
F32 = jnp.float32


def normalize_rows(vectors):
    radius = jnp.sqrt(jnp.sum(vectors * vectors, axis=1, keepdims=True) + epsilon)
    return (vectors / radius, radius)


def projection_backward(unit_vectors, radius, gradient):
    inner = jnp.sum(unit_vectors * gradient, axis=1, keepdims=True)
    return (gradient - unit_vectors * inner) / radius


def kernel(
    S,
    B,
    scale_ref,
    bias_ref,
    req_ref,
    hot_ref,
    cold_ref,
    lines_ref,
    parent_ref,
    pos_ref,
    tally_ref,
    dq_ref,
    hotg_ref,
    coldg_ref,
    keys,
    coldb,
    ysend,
    yrecv,
    zsend,
    zrecv,
    queries,
    qsend,
    qrecv,
    qunit,
    qdir,
    grads,
    coldacc,
    csend,
    crecv,
    hotacc,
    hpart,
    hfull,
    sem_ks,
    sem_kr,
    sem_ys,
    sem_yr,
    sem_zs,
    sem_zr,
    sem_qs,
    sem_qr,
    sem_ps,
    sem_pr,
    sem_gz,
    sem_gy,
    sem_gc,
    sem_gr,
    sem_cs,
    sem_cr,
    sem_xs,
    sem_xr,
    sem_hz,
    sem_hy,
    sem_hc,
    sem_hr,
):
    S2, B2, U = S // 2, B // 2, 2 * S
    pairs, width = req_ref.shape
    rows = cold_ref.shape[0]
    hot_rows = hot_ref.shape[0]
    HB = lines_ref.shape[1]
    CB = parent_ref.shape[1]
    RB = rows // B
    HR = hot_rows // U
    s = lax.axis_index("shard")
    b = lax.axis_index("blk")
    line, y = s // 2, lax.rem(s, 2)
    x, c = b // 2, lax.rem(b, 2)
    u = s * 2 + c
    ypart = line * 2 + (1 - y)
    cpart = x * 2 + (1 - c)
    dot = functools.partial(lax.dot_general, preferred_element_type=F32)

    def send(src, dst, ss, rs, sh, bl):
        return pltpu.make_async_remote_copy(
            src_ref=src,
            dst_ref=dst,
            send_sem=ss,
            recv_sem=rs,
            device_id=(sh, bl),
            device_id_type=pl.DeviceIdType.MESH,
        )

    def loop(lo, hi, f):
        def body(i, carry):
            f(i)
            return carry

        lax.fori_loop(lo, hi, body, 0)

    barrier = pltpu.get_barrier_semaphore()

    def greet(k):
        v = lax.rem(u + k, U)
        pl.semaphore_signal(
            barrier,
            inc=1,
            device_id=(v // 2, x * 2 + lax.rem(v, 2)),
            device_id_type=pl.DeviceIdType.MESH,
        )

    loop(1, U, greet)

    def greet_blk(k):
        xo = lax.rem(x + k, B2)
        for cc in range(2):
            pl.semaphore_signal(
                barrier, inc=1, device_id=(s, xo * 2 + cc), device_id_type=pl.DeviceIdType.MESH
            )

    loop(1, B2, greet_blk)

    slot = lax.broadcasted_iota(jnp.int32, (pairs, CB), 1)
    cold_key = jnp.where(slot < tally_ref[...], parent_ref[...] * rows + pos_ref[...], -1)
    both = jnp.concatenate(
        [lines_ref[...], cold_key, jnp.zeros((pairs, 128 - HB - CB), jnp.int32)], axis=1
    )
    keys[u] = jnp.transpose(both)[:8, :]

    qf = req_ref[...].astype(F32)
    q_unit, q_radius = normalize_rows(qf)
    qunit[...] = q_unit
    queries[b] = q_unit.astype(BF)

    pl.semaphore_wait(barrier, U - 1 + 2 * (B2 - 1))

    def key_copy(src_u, k, v):
        return send(
            keys.at[src_u],
            keys.at[src_u],
            sem_ks.at[k],
            sem_kr.at[src_u],
            v // 2,
            x * 2 + lax.rem(v, 2),
        )

    def send_keys(k):
        v = lax.rem(u + k, U)
        key_copy(u, k, v).start()

    loop(1, U, send_keys)

    def q_copy(slot_b, k, bo):
        return send(
            queries.at[slot_b], queries.at[slot_b], sem_qs.at[k], sem_qr.at[slot_b], s, bo
        )

    loop(1, B, lambda k: q_copy(b, k, lax.rem(b + k, B)).start())

    coldb[...] = cold_ref[...].astype(BF)

    def own_index(v):
        block = keys[v]
        rel = block[HB : HB + CB, :] - s * rows
        good = (rel >= 0) & (rel < rows) & (block[HB : HB + CB, :] >= 0)
        return jnp.max(jnp.where(good, rel, -1), axis=0, keepdims=True)

    def lookup(p):
        idx = own_index(p * 2 + c)
        col = jnp.transpose(jnp.broadcast_to(idx, (128, pairs)))[:, :1]
        hit = lax.broadcasted_iota(jnp.int32, (pairs, rows), 1) == col
        return dot(hit.astype(F32).astype(BF), coldb[...], (((1,), (0,)), ((), ())))

    def y_copy(lo):
        return send(ysend.at[lo], yrecv.at[lo], sem_ys.at[lo], sem_yr.at[lo], ypart, b)

    def z_copy(src, dst, lo):
        return send(zsend.at[src], zrecv.at[dst], sem_zs.at[src], sem_zr.at[dst], lo * 2 + y, b)

    def wait_key(v):
        key_copy(v, 0, v).wait_recv()

    def fetch_y(k):
        lo = lax.rem(line + k, S2)
        p = lo * 2 + (1 - y)
        wait_key(p * 2 + c)
        ysend[lo] = lookup(p).astype(BF)
        y_copy(lo).start()

    loop(1, S2 + 1, fetch_y)

    def fetch_z(k):
        lo = lax.rem(line + k, S2)
        p = lo * 2 + y
        wait_key(p * 2 + c)
        part = lookup(p)
        y_copy(lo).wait_recv()
        zsend[lo] = (part + yrecv[lo].astype(F32)).astype(BF)
        z_copy(lo, line, lo).start()

    loop(1, S2, fetch_z)

    lines = lines_ref[...]
    hot_iota = lax.broadcasted_iota(jnp.int32, (pairs, hot_rows), 1)
    counts = jnp.zeros((pairs, hot_rows), F32)
    for h in range(HB):
        counts = counts + (hot_iota == lines[:, h : h + 1]).astype(F32)
    item = dot(counts.astype(BF), hot_ref[...], (((1,), (0,)), ((), ())))
    item = item + lookup(s)
    y_copy(line).wait_recv()
    item = item + yrecv[line].astype(F32)

    def take_z(k, acc):
        lo = lax.rem(line + S2 - k, S2)
        z_copy(line, lo, lo).wait_recv()
        return acc + zrecv[lo].astype(F32)

    item = lax.fori_loop(1, S2, take_z, item)

    unit, radius = normalize_rows(item)
    low = unit.astype(BF)
    scale = scale_ref[0]
    bias = bias_ref[0]
    diag = lax.broadcasted_iota(jnp.int32, (pairs, pairs), 0) == lax.broadcasted_iota(
        jnp.int32, (pairs, pairs), 1
    )

    def pair_grads(q, positive):
        logits = scale * dot(low, q, (((1,), (1,)), ((), ()))) + bias
        g = jax.nn.sigmoid(logits)
        if positive:
            g = g - diag.astype(F32)
        g = g.astype(BF)
        return dot(g, q, (((1,), (0,)), ((), ()))), dot(g, low, (((0,), (0,)), ((), ())))

    item_dir, own_qdir = pair_grads(queries[b], True)
    qdir[...] = own_qdir

    def p_copy(bo, dst):
        return send(qsend.at[bo], qrecv.at[dst], sem_ps.at[bo], sem_pr.at[dst], s, bo)

    def loss_block(k, acc):
        bo = lax.rem(b + k, B)
        q_copy(bo, 0, bo).wait_recv()
        add, part = pair_grads(queries[bo], False)
        qsend[bo] = part.astype(BF)
        p_copy(bo, b).start()
        return acc + add

    item_dir = lax.fori_loop(1, B, loss_block, item_dir)
    grads[u] = projection_backward(unit, radius, scale * item_dir).astype(BF)

    def gz_copy(v, lo):
        return send(grads.at[v], grads.at[v], sem_gz.at[lo], sem_gr.at[v], lo * 2 + y, b)

    def gy_copy(v, lo):
        return send(grads.at[v], grads.at[v], sem_gy.at[lo], sem_gr.at[v], ypart, b)

    def gc_copy(v, p):
        return send(grads.at[v], grads.at[v], sem_gc.at[p], sem_gr.at[v], s, cpart)

    loop(1, S2, lambda k: gz_copy(u, lax.rem(line + k, S2)).start())

    coldacc[...] = jnp.zeros(coldacc.shape, F32)
    hotacc[...] = jnp.zeros(hotacc.shape, F32)
    row_iota = lax.broadcasted_iota(jnp.int32, (RB, pairs), 0)
    hrow_iota = lax.broadcasted_iota(jnp.int32, (HR, pairs), 0) + u * HR

    def consume(v):
        g = grads[v]
        idx = own_index(v)
        block = keys[v]
        cnt = jnp.zeros((HR, pairs), F32)
        for h in range(HB):
            cnt = cnt + (hrow_iota == block[h : h + 1, :]).astype(F32)
        hotacc[...] += dot(cnt.astype(BF), g, (((1,), (0,)), ((), ())))

        def part(xo):
            hit = (row_iota == idx - (xo * 2 + c) * RB).astype(F32).astype(BF)
            coldacc[xo] += dot(hit, g, (((1,), (0,)), ((), ())))

        loop(0, B2, part)

    def own_column(k):
        lo = lax.rem(line + S2 - k, S2)
        p = lo * 2 + y
        v = p * 2 + c

        @pl.when(k > 0)
        def _():
            gz_copy(v, lo).wait_recv()

        gy_copy(v, lo).start()
        gc_copy(v, p).start()
        consume(v)

    loop(0, S2, own_column)

    def y_column(k):
        lo = lax.rem(line + S2 - k, S2)
        p = lo * 2 + (1 - y)
        v = p * 2 + c
        gy_copy(v, lo).wait_recv()
        gc_copy(v, p).start()
        consume(v)

    loop(0, S2, y_column)

    def core_column(k):
        p = lax.rem(s + S - k, S)
        v = p * 2 + (1 - c)
        wait_key(v)
        gc_copy(v, p).wait_recv()
        consume(v)

    loop(0, S, core_column)

    def x_copy(dst, xo):
        return send(
            hpart.at[x], hpart.at[dst], sem_xs.at[xo], sem_xr.at[dst], s, xo * 2 + c
        )

    hpart[x] = hotacc[...].astype(BF)
    loop(1, B2, lambda k: x_copy(x, lax.rem(x + k, B2)).start())

    def c_copy(src, dst):
        return send(
            csend.at[src], crecv.at[dst], sem_cs.at[src], sem_cr.at[dst], s, src * 2 + c
        )

    def send_cold(k):
        xo = lax.rem(x + k, B2)
        csend[xo] = coldacc[xo].astype(BF)
        c_copy(xo, x).start()

    loop(1, B2, send_cold)

    def wait_x(k):
        xo = lax.rem(x + k, B2)
        x_copy(xo, xo).wait_recv()

    loop(1, B2, wait_x)
    total = hpart[0].astype(F32)
    for xo in range(1, B2):
        total = total + hpart[xo].astype(F32)
    hfull[u] = total.astype(BF)

    def hz_copy(v, lo):
        return send(hfull.at[v], hfull.at[v], sem_hz.at[lo], sem_hr.at[v], lo * 2 + y, b)

    def hy_copy(v, lo):
        return send(hfull.at[v], hfull.at[v], sem_hy.at[lo], sem_hr.at[v], ypart, b)

    def hc_copy(v, p):
        return send(hfull.at[v], hfull.at[v], sem_hc.at[p], sem_hr.at[v], s, cpart)

    loop(1, S2, lambda k: hz_copy(u, lax.rem(line + k, S2)).start())
    hy_copy(u, line).start()
    hc_copy(u, s).start()

    def take_p(k, acc):
        bo = lax.rem(b + k, B)
        p_copy(bo, bo).wait_recv()
        return acc + qrecv[bo].astype(F32)

    q_total = lax.fori_loop(1, B, take_p, qdir[...])
    _, q_radius2 = normalize_rows(req_ref[...].astype(F32))
    dq_ref[...] = projection_backward(qunit[...], q_radius2, scale * q_total)

    def hot_line(k):
        lo = lax.rem(line + S2 - k, S2)
        p = lo * 2 + y
        v = p * 2 + c
        hz_copy(v, lo).wait_recv()
        hy_copy(v, lo).start()
        hc_copy(v, p).start()

    loop(1, S2, hot_line)

    def hot_y(k):
        lo = lax.rem(line + S2 - k, S2)
        p = lo * 2 + (1 - y)
        v = p * 2 + c
        hy_copy(v, lo).wait_recv()
        hc_copy(v, p).start()

    loop(0, S2, hot_y)

    def take_cold(k, acc):
        xo = lax.rem(x + k, B2)
        c_copy(xo, xo).wait_recv()
        return acc + crecv[xo].astype(F32)

    coldg_ref[...] = lax.fori_loop(1, B2, take_cold, coldacc[x])

    def hot_core(k):
        p = lax.rem(s + S - k, S)
        hc_copy(p * 2 + (1 - c), p).wait_recv()

    loop(0, S, hot_core)
    hotg_ref[...] = hfull[...]

    loop(1, U, lambda k: key_copy(u, k, lax.rem(u + k, U)).wait_send())
    loop(1, B, lambda k: q_copy(b, k, lax.rem(b + k, B)).wait_send())
    loop(0, S2, lambda lo: y_copy(lo).wait_send())

    def sent_line(k):
        lo = lax.rem(line + k, S2)
        z_copy(lo, line, lo).wait_send()
        gz_copy(u, lo).wait_send()
        hz_copy(u, lo).wait_send()

    loop(1, S2, sent_line)
    loop(1, B, lambda k: p_copy(lax.rem(b + k, B), b).wait_send())

    def sent_y(lo):
        gy_copy((lo * 2 + y) * 2 + c, lo).wait_send()
        hy_copy((lo * 2 + y) * 2 + c, lo).wait_send()

    loop(0, S2, sent_y)

    def sent_c(p):
        gc_copy(p * 2 + c, p).wait_send()
        hc_copy(p * 2 + c, p).wait_send()

    loop(0, S, sent_c)

    def sent_x(k):
        xo = lax.rem(x + k, B2)
        x_copy(x, xo).wait_send()
        c_copy(xo, x).wait_send()

    loop(1, B2, sent_x)


def body(
    request_embeddings,
    frequent_entry_matrix,
    rare_entry_matrix,
    frequent_entry_lines,
    rare_place_parent,
    rare_local_position,
    rare_place_tally,
    sharpness_factor,
    pairscore_additive,
):
    pairs, width = request_embeddings.shape
    S = lax.axis_size("shard")
    B = lax.axis_size("blk")
    rows = rare_entry_matrix.shape[0]
    hot_rows = frequent_entry_matrix.shape[0]
    S2, B2, U = S // 2, B // 2, 2 * S
    RB, HR = rows // B, hot_rows // U
    vmem = pl.BlockSpec(memory_space=pltpu.VMEM)
    smem = pl.BlockSpec(memory_space=pltpu.SMEM)
    dma = lambda n: pltpu.SemaphoreType.DMA((n,))
    blocks = lambda n, dtype: pltpu.VMEM((n, pairs, width), dtype)
    dq, hot, cold = pl.pallas_call(
        functools.partial(kernel, S, B),
        out_shape=(
            jax.ShapeDtypeStruct((pairs, width), F32),
            jax.ShapeDtypeStruct((U, HR, width), BF),
            jax.ShapeDtypeStruct((RB, width), F32),
        ),
        in_specs=[smem, smem] + [vmem] * 7,
        out_specs=(vmem, vmem, vmem),
        scratch_shapes=[
            pltpu.VMEM((U, 8, pairs), jnp.int32),
            pltpu.VMEM((rows, width), BF),
            blocks(S2, BF),
            blocks(S2, BF),
            blocks(S2, BF),
            blocks(S2, BF),
            blocks(B, BF),
            blocks(B, BF),
            blocks(B, BF),
            pltpu.VMEM((pairs, width), F32),
            pltpu.VMEM((pairs, width), F32),
            blocks(U, BF),
            pltpu.VMEM((B2, RB, width), F32),
            pltpu.VMEM((B2, RB, width), BF),
            pltpu.VMEM((B2, RB, width), BF),
            pltpu.VMEM((HR, width), F32),
            pltpu.VMEM((B2, HR, width), BF),
            pltpu.VMEM((U, HR, width), BF),
            dma(U),
            dma(U),
            dma(S2),
            dma(S2),
            dma(S2),
            dma(S2),
            dma(B),
            dma(B),
            dma(B),
            dma(B),
            dma(S2),
            dma(S2),
            dma(S),
            dma(U),
            dma(B2),
            dma(B2),
            dma(B2),
            dma(B2),
            dma(S2),
            dma(S2),
            dma(S),
            dma(U),
        ],
        compiler_params=pltpu.CompilerParams(
            collective_id=0, has_side_effects=True, vmem_limit_bytes=56 * 1024 * 1024
        ),
    )(
        sharpness_factor,
        pairscore_additive,
        request_embeddings,
        frequent_entry_matrix,
        rare_entry_matrix,
        frequent_entry_lines,
        rare_place_parent,
        rare_local_position,
        rare_place_tally.reshape(pairs, 1),
    )
    return dq, hot.reshape(hot_rows, width).astype(F32), cold


def solution(mesh):
    in_specs = (
        P(("shard", "blk"), None),
        P(),
        P("shard", None),
        P(("shard", "blk"), None),
        P(("shard", "blk"), None),
        P(("shard", "blk"), None),
        P(("shard", "blk")),
        P(),
        P(),
    )
    out_specs = (P(("shard", "blk"), None), P(), P(("shard", "blk"), None))
    return jax.shard_map(body, mesh=mesh, in_specs=in_specs, out_specs=out_specs, check_vma=False)
```

```python
import functools

import jax
import jax.numpy as jnp
from jax import lax
from jax.experimental import pallas as pl
from jax.experimental.pallas import tpu as pltpu
from jax.sharding import PartitionSpec as P

epsilon = 1e-06
BF = jnp.bfloat16
F32 = jnp.float32


def normalize_rows(vectors):
    radius = jnp.sqrt(jnp.sum(vectors * vectors, axis=1, keepdims=True) + epsilon)
    return (vectors / radius, radius)


def projection_backward(unit_vectors, radius, gradient):
    inner = jnp.sum(unit_vectors * gradient, axis=1, keepdims=True)
    return (gradient - unit_vectors * inner) / radius


def kernel(
    S,
    B,
    scale_ref,
    bias_ref,
    req_ref,
    hot_ref,
    cold_ref,
    lines_ref,
    parent_ref,
    pos_ref,
    tally_ref,
    dq_ref,
    hotg_ref,
    coldg_ref,
    keys,
    coldb,
    ysend,
    yrecv,
    zsend,
    zrecv,
    queries,
    qsend,
    qrecv,
    qunit,
    qdir,
    grads,
    coldacc,
    csend,
    crecv,
    hotacc,
    hpart,
    hfull,
    sem_ks,
    sem_kr,
    sem_ys,
    sem_yr,
    sem_zs,
    sem_zr,
    sem_qs,
    sem_qr,
    sem_ps,
    sem_pr,
    sem_gz,
    sem_gy,
    sem_gc,
    sem_gr,
    sem_cs,
    sem_cr,
    sem_xs,
    sem_xr,
    sem_hz,
    sem_hy,
    sem_hc,
    sem_hr,
):
    S2, B2, U = S // 2, B // 2, 2 * S
    pairs, width = req_ref.shape
    rows = cold_ref.shape[0]
    hot_rows = hot_ref.shape[0]
    HB = lines_ref.shape[0]
    CB = parent_ref.shape[0]
    RB = rows // B
    HR = hot_rows // U
    s = lax.axis_index("shard")
    b = lax.axis_index("blk")
    line, y = s // 2, lax.rem(s, 2)
    x, c = b // 2, lax.rem(b, 2)
    u = s * 2 + c
    G = 4 if S2 % 4 == 0 else 1

    def place(p, cc):
        return (cc * 2 + lax.rem(p, 2)) * S2 + p // 2

    w = place(s, c)
    ypart = line * 2 + (1 - y)
    cpart = x * 2 + (1 - c)
    dot = functools.partial(lax.dot_general, preferred_element_type=F32)

    def send(src, dst, ss, rs, sh, bl):
        return pltpu.make_async_remote_copy(
            src_ref=src,
            dst_ref=dst,
            send_sem=ss,
            recv_sem=rs,
            device_id=(sh, bl),
            device_id_type=pl.DeviceIdType.MESH,
        )

    def loop(lo, hi, f):
        def body(i, carry):
            f(i)
            return carry

        lax.fori_loop(lo, hi, body, 0)

    barrier = pltpu.get_barrier_semaphore()

    def greet(k):
        v = lax.rem(u + k, U)
        pl.semaphore_signal(
            barrier,
            inc=1,
            device_id=(v // 2, x * 2 + lax.rem(v, 2)),
            device_id_type=pl.DeviceIdType.MESH,
        )

    loop(1, U, greet)

    def greet_blk(k):
        xo = lax.rem(x + k, B2)
        for cc in range(2):
            pl.semaphore_signal(
                barrier, inc=1, device_id=(s, xo * 2 + cc), device_id_type=pl.DeviceIdType.MESH
            )

    loop(1, B2, greet_blk)

    slot = lax.broadcasted_iota(jnp.int32, (CB, pairs), 0)
    cold_key = jnp.where(slot < tally_ref[...], parent_ref[...] * rows + pos_ref[...], -1)
    keys[w] = jnp.concatenate([lines_ref[...], cold_key], axis=0)

    qf = req_ref[...].astype(F32)
    q_unit, q_radius = normalize_rows(qf)
    qunit[...] = q_unit
    queries[b] = q_unit.astype(BF)

    pl.semaphore_wait(barrier, U - 1 + 2 * (B2 - 1))

    def key_copy(src_w, k, p, cc):
        return send(keys.at[src_w], keys.at[src_w], sem_ks.at[k], sem_kr.at[src_w], p, x * 2 + cc)

    def send_keys(k):
        key_copy(w, k, lax.rem(s + k, S), c).start()

    def send_keys_core(k):
        key_copy(w, S + k, lax.rem(s + k, S), 1 - c).start()

    loop(1, S, send_keys)
    loop(0, S, send_keys_core)

    def q_copy(slot_b, k, bo):
        return send(
            queries.at[slot_b], queries.at[slot_b], sem_qs.at[k], sem_qr.at[slot_b], s, bo
        )

    loop(1, B, lambda k: q_copy(b, k, lax.rem(b + k, B)).start())

    coldb[...] = cold_ref[...].astype(BF)

    def one_hot(where, idx):
        same = where.astype(jnp.int16) == idx.astype(jnp.int16)
        return jnp.where(same, jnp.ones((), BF), jnp.zeros((), BF))

    def own_index(block):
        rel = block[HB : HB + CB, :] - s * rows
        good = (rel >= 0) & (rel < rows) & (block[HB : HB + CB, :] >= 0)
        return jnp.max(jnp.where(good, rel, -1), axis=0, keepdims=True)

    def lookup(p):
        idx = own_index(keys[place(p, c)])
        col = jnp.transpose(jnp.broadcast_to(idx, (128, pairs)))[:, :1]
        hit = one_hot(lax.broadcasted_iota(jnp.int32, (pairs, rows), 1), col)
        return dot(hit, coldb[...], (((1,), (0,)), ((), ())))

    def y_copy(lo):
        return send(ysend.at[lo], yrecv.at[lo], sem_ys.at[lo], sem_yr.at[lo], ypart, b)

    def z_copy(src, dst, lo):
        return send(zsend.at[src], zrecv.at[dst], sem_zs.at[src], sem_zr.at[dst], lo * 2 + y, b)

    def wait_key(p, cc):
        key_copy(place(p, cc), 0, p, cc).wait_recv()

    def fetch_y(k):
        lo = lax.rem(line + k, S2)
        p = lo * 2 + (1 - y)
        wait_key(p, c)
        ysend[lo] = lookup(p).astype(BF)
        y_copy(lo).start()

    loop(1, S2 + 1, fetch_y)

    def fetch_z(k):
        lo = lax.rem(line + k, S2)
        p = lo * 2 + y
        wait_key(p, c)
        part = lookup(p)
        y_copy(lo).wait_recv()
        zsend[lo] = (part + yrecv[lo].astype(F32)).astype(BF)
        z_copy(lo, line, lo).start()

    loop(1, S2, fetch_z)

    own_keys = jnp.concatenate([keys[w]] * (128 // (HB + CB)), axis=0)
    lines = jnp.transpose(own_keys)
    hot_iota = lax.broadcasted_iota(jnp.int32, (pairs, hot_rows), 1)
    counts = jnp.zeros((pairs, hot_rows), BF)
    for h in range(HB):
        counts = counts + one_hot(hot_iota, lines[:, h : h + 1])
    item = dot(counts, hot_ref[...], (((1,), (0,)), ((), ())))
    item = item + lookup(s)
    y_copy(line).wait_recv()
    item = item + yrecv[line].astype(F32)

    def take_z(k, acc):
        lo = lax.rem(line + S2 - k, S2)
        z_copy(line, lo, lo).wait_recv()
        return acc + zrecv[lo].astype(F32)

    item = lax.fori_loop(1, S2, take_z, item)

    unit, radius = normalize_rows(item)
    low = unit.astype(BF)
    scale = scale_ref[0]
    bias = bias_ref[0]
    diag = lax.broadcasted_iota(jnp.int32, (pairs, pairs), 0) == lax.broadcasted_iota(
        jnp.int32, (pairs, pairs), 1
    )

    def pair_grads(q, positive):
        logits = scale * dot(low, q, (((1,), (1,)), ((), ()))) + bias
        g = jax.nn.sigmoid(logits)
        if positive:
            g = g - diag.astype(F32)
        g = g.astype(BF)
        return dot(g, q, (((1,), (0,)), ((), ()))), dot(g, low, (((0,), (0,)), ((), ())))

    item_dir, own_qdir = pair_grads(queries[b], True)
    qdir[...] = own_qdir

    def p_copy(bo, dst):
        return send(qsend.at[bo], qrecv.at[dst], sem_ps.at[bo], sem_pr.at[dst], s, bo)

    def loss_block(k, acc):
        bo = lax.rem(b + k, B)
        q_copy(bo, 0, bo).wait_recv()
        add, part = pair_grads(queries[bo], False)
        qsend[bo] = part.astype(BF)
        p_copy(bo, b).start()
        return acc + add

    item_dir = lax.fori_loop(1, B, loss_block, item_dir)
    grads[w] = projection_backward(unit, radius, scale * item_dir).astype(BF)

    def gz_copy(v, lo):
        return send(grads.at[v], grads.at[v], sem_gz.at[lo], sem_gr.at[v], lo * 2 + y, b)

    def gy_copy(v, lo):
        return send(grads.at[v], grads.at[v], sem_gy.at[lo], sem_gr.at[v], ypart, b)

    def gc_copy(v, p):
        return send(grads.at[v], grads.at[v], sem_gc.at[p], sem_gr.at[v], s, cpart)

    loop(1, S2, lambda k: gz_copy(w, lax.rem(line + k, S2)).start())
    gy_copy(w, line).start()
    gc_copy(w, s).start()

    coldacc[...] = jnp.zeros(coldacc.shape, F32)
    hotacc[...] = jnp.zeros(hotacc.shape, F32)
    row_iota = lax.broadcasted_iota(jnp.int32, (RB, G * pairs), 0)
    hrow_iota = lax.broadcasted_iota(jnp.int32, (HR, G * pairs), 0)

    def group_rows(first):
        return jnp.concatenate([grads[first + i] for i in range(G)], axis=0)

    def add_hot(group):
        def chunk(i):
            first = group * S2 + i * G
            ids = jnp.concatenate([keys[first + j][:HB, :] for j in range(G)], axis=1) - u * HR
            ids = jnp.where((ids >= 0) & (ids < HR), ids, -1)
            cnt = jnp.zeros((HR, G * pairs), BF)
            for h in range(HB):
                cnt = cnt + one_hot(hrow_iota, ids[h : h + 1, :])
            hotacc[...] += dot(cnt, group_rows(first), (((1,), (0,)), ((), ())))

        loop(0, S2 // G, chunk)

    def add_cold(group, xo):
        def chunk(i):
            first = group * S2 + i * G
            ids = jnp.concatenate([own_index(keys[first + j]) for j in range(G)], axis=1)
            hit = one_hot(row_iota, ids - (xo * 2 + c) * RB)
            coldacc[xo] += dot(hit, group_rows(first), (((1,), (0,)), ((), ())))

        loop(0, S2 // G, chunk)

    def line_column(k):
        lo = lax.rem(line + S2 - k, S2)
        p = lo * 2 + y
        v = place(p, c)
        gz_copy(v, lo).wait_recv()
        gy_copy(v, lo).start()
        gc_copy(v, p).start()

    loop(1, S2, line_column)
    mine, other = c * 2, (1 - c) * 2
    add_hot(mine + y)
    loop(0, B2, lambda xo: add_cold(mine + y, xo))

    def y_column(k):
        lo = lax.rem(line + S2 - k, S2)
        p = lo * 2 + (1 - y)
        v = place(p, c)
        gy_copy(v, lo).wait_recv()
        gc_copy(v, p).start()

    loop(0, S2, y_column)

    def core_column(yy):
        def one(k):
            p = lax.rem(line + S2 - k, S2) * 2 + yy
            wait_key(p, 1 - c)
            gc_copy(place(p, 1 - c), p).wait_recv()

        loop(0, S2, one)

    core_column(y)
    for group in (other + y, mine + 1 - y):
        add_hot(group)
        loop(0, B2, functools.partial(add_cold, group))
    core_column(1 - y)
    last = other + 1 - y
    add_hot(last)

    def x_copy(dst, xo):
        return send(
            hpart.at[x], hpart.at[dst], sem_xs.at[xo], sem_xr.at[dst], s, xo * 2 + c
        )

    hpart[x] = hotacc[...].astype(BF)
    loop(1, B2, lambda k: x_copy(x, lax.rem(x + k, B2)).start())

    def c_copy(src, dst):
        return send(
            csend.at[src], crecv.at[dst], sem_cs.at[src], sem_cr.at[dst], s, src * 2 + c
        )

    def send_cold(k):
        xo = lax.rem(x + k, B2)
        add_cold(last, xo)
        csend[xo] = coldacc[xo].astype(BF)
        c_copy(xo, x).start()

    loop(1, B2, send_cold)

    def wait_x(k):
        xo = lax.rem(x + k, B2)
        x_copy(xo, xo).wait_recv()

    loop(1, B2, wait_x)
    total = hpart[0].astype(F32)
    for xo in range(1, B2):
        total = total + hpart[xo].astype(F32)
    hfull[u] = total.astype(BF)

    def hz_copy(v, lo):
        return send(hfull.at[v], hfull.at[v], sem_hz.at[lo], sem_hr.at[v], lo * 2 + y, b)

    def hy_copy(v, lo):
        return send(hfull.at[v], hfull.at[v], sem_hy.at[lo], sem_hr.at[v], ypart, b)

    def hc_copy(v, p):
        return send(hfull.at[v], hfull.at[v], sem_hc.at[p], sem_hr.at[v], s, cpart)

    loop(1, S2, lambda k: hz_copy(u, lax.rem(line + k, S2)).start())
    hy_copy(u, line).start()
    hc_copy(u, s).start()

    add_cold(last, x)

    def take_p(k, acc):
        bo = lax.rem(b + k, B)
        p_copy(bo, bo).wait_recv()
        return acc + qrecv[bo].astype(F32)

    q_total = lax.fori_loop(1, B, take_p, qdir[...])
    _, q_radius2 = normalize_rows(req_ref[...].astype(F32))
    dq_ref[...] = projection_backward(qunit[...], q_radius2, scale * q_total)

    def hot_line(k):
        lo = lax.rem(line + S2 - k, S2)
        p = lo * 2 + y
        v = p * 2 + c
        hz_copy(v, lo).wait_recv()
        hy_copy(v, lo).start()
        hc_copy(v, p).start()

    loop(1, S2, hot_line)

    def hot_y(k):
        lo = lax.rem(line + S2 - k, S2)
        p = lo * 2 + (1 - y)
        v = p * 2 + c
        hy_copy(v, lo).wait_recv()
        hc_copy(v, p).start()

    loop(0, S2, hot_y)

    def take_cold(k, acc):
        xo = lax.rem(x + k, B2)
        c_copy(xo, xo).wait_recv()
        return acc + crecv[xo].astype(F32)

    coldg_ref[...] = lax.fori_loop(1, B2, take_cold, coldacc[x])

    def hot_core(k):
        p = lax.rem(s + S - k, S)
        hc_copy(p * 2 + (1 - c), p).wait_recv()

    loop(0, S, hot_core)
    hotg_ref[...] = hfull[...]

    loop(1, S, lambda k: key_copy(w, k, lax.rem(s + k, S), c).wait_send())
    loop(0, S, lambda k: key_copy(w, S + k, lax.rem(s + k, S), 1 - c).wait_send())
    loop(1, B, lambda k: q_copy(b, k, lax.rem(b + k, B)).wait_send())
    loop(0, S2, lambda lo: y_copy(lo).wait_send())

    def sent_line(k):
        lo = lax.rem(line + k, S2)
        z_copy(lo, line, lo).wait_send()
        gz_copy(w, lo).wait_send()
        hz_copy(u, lo).wait_send()

    loop(1, S2, sent_line)
    loop(1, B, lambda k: p_copy(lax.rem(b + k, B), b).wait_send())

    def sent_y(lo):
        gy_copy(place(lo * 2 + y, c), lo).wait_send()
        hy_copy((lo * 2 + y) * 2 + c, lo).wait_send()

    loop(0, S2, sent_y)

    def sent_c(p):
        gc_copy(place(p, c), p).wait_send()
        hc_copy(p * 2 + c, p).wait_send()

    loop(0, S, sent_c)

    def sent_x(k):
        xo = lax.rem(x + k, B2)
        x_copy(x, xo).wait_send()
        c_copy(xo, x).wait_send()

    loop(1, B2, sent_x)


def body(
    request_embeddings,
    frequent_entry_matrix,
    rare_entry_matrix,
    frequent_entry_lines,
    rare_place_parent,
    rare_local_position,
    rare_place_tally,
    sharpness_factor,
    pairscore_additive,
):
    pairs, width = request_embeddings.shape
    S = lax.axis_size("shard")
    B = lax.axis_size("blk")
    rows = rare_entry_matrix.shape[0]
    hot_rows = frequent_entry_matrix.shape[0]
    S2, B2, U = S // 2, B // 2, 2 * S
    RB, HR = rows // B, hot_rows // U
    ids = frequent_entry_lines.shape[1] + rare_place_parent.shape[1]
    vmem = pl.BlockSpec(memory_space=pltpu.VMEM)
    smem = pl.BlockSpec(memory_space=pltpu.SMEM)
    dma = lambda n: pltpu.SemaphoreType.DMA((n,))
    blocks = lambda n, dtype: pltpu.VMEM((n, pairs, width), dtype)
    dq, hot, cold = pl.pallas_call(
        functools.partial(kernel, S, B),
        out_shape=(
            jax.ShapeDtypeStruct((pairs, width), F32),
            jax.ShapeDtypeStruct((U, HR, width), BF),
            jax.ShapeDtypeStruct((RB, width), F32),
        ),
        in_specs=[smem, smem] + [vmem] * 7,
        out_specs=(vmem, vmem, vmem),
        scratch_shapes=[
            pltpu.VMEM((U, ids, pairs), jnp.int32),
            pltpu.VMEM((rows, width), BF),
            blocks(S2, BF),
            blocks(S2, BF),
            blocks(S2, BF),
            blocks(S2, BF),
            blocks(B, BF),
            blocks(B, BF),
            blocks(B, BF),
            pltpu.VMEM((pairs, width), F32),
            pltpu.VMEM((pairs, width), F32),
            blocks(U, BF),
            pltpu.VMEM((B2, RB, width), F32),
            pltpu.VMEM((B2, RB, width), BF),
            pltpu.VMEM((B2, RB, width), BF),
            pltpu.VMEM((HR, width), F32),
            pltpu.VMEM((B2, HR, width), BF),
            pltpu.VMEM((U, HR, width), BF),
            dma(U),
            dma(U),
            dma(S2),
            dma(S2),
            dma(S2),
            dma(S2),
            dma(B),
            dma(B),
            dma(B),
            dma(B),
            dma(S2),
            dma(S2),
            dma(S),
            dma(U),
            dma(B2),
            dma(B2),
            dma(B2),
            dma(B2),
            dma(S2),
            dma(S2),
            dma(S),
            dma(U),
        ],
        compiler_params=pltpu.CompilerParams(
            collective_id=0, has_side_effects=True, vmem_limit_bytes=56 * 1024 * 1024
        ),
    )(
        sharpness_factor,
        pairscore_additive,
        request_embeddings,
        frequent_entry_matrix,
        rare_entry_matrix,
        frequent_entry_lines.T,
        rare_place_parent.T,
        rare_local_position.T,
        rare_place_tally.reshape(1, pairs),
    )
    return dq, hot.reshape(hot_rows, width).astype(F32), cold


def solution(mesh):
    in_specs = (
        P(("shard", "blk"), None),
        P(),
        P("shard", None),
        P(("shard", "blk"), None),
        P(("shard", "blk"), None),
        P(("shard", "blk"), None),
        P(("shard", "blk")),
        P(),
        P(),
    )
    out_specs = (P(("shard", "blk"), None), P(), P(("shard", "blk"), None))
    return jax.shard_map(body, mesh=mesh, in_specs=in_specs, out_specs=out_specs, check_vma=False)
```

```python
import functools

import jax
import jax.numpy as jnp
from jax import lax
from jax.experimental import pallas as pl
from jax.experimental.pallas import tpu as pltpu
from jax.sharding import PartitionSpec as P

epsilon = 1e-06
BF = jnp.bfloat16
F32 = jnp.float32


def normalize_rows(vectors):
    radius = jnp.sqrt(jnp.sum(vectors * vectors, axis=1, keepdims=True) + epsilon)
    return (vectors / radius, radius)


def projection_backward(unit_vectors, radius, gradient):
    inner = jnp.sum(unit_vectors * gradient, axis=1, keepdims=True)
    return (gradient - unit_vectors * inner) / radius


def kernel(
    S,
    B,
    scale_ref,
    bias_ref,
    req_ref,
    hot_ref,
    cold_ref,
    lines_ref,
    parent_ref,
    pos_ref,
    tally_ref,
    dq_ref,
    hotg_ref,
    coldg_ref,
    keys,
    coldb,
    ysend,
    yrecv,
    zsend,
    zrecv,
    queries,
    qsend,
    qrecv,
    qunit,
    qdir,
    grads,
    coldacc,
    csend,
    crecv,
    hotacc,
    hpart,
    hfull,
    sem_ks,
    sem_kr,
    sem_ys,
    sem_yr,
    sem_zs,
    sem_zr,
    sem_qs,
    sem_qr,
    sem_ps,
    sem_pr,
    sem_gz,
    sem_gy,
    sem_gc,
    sem_gr,
    sem_cs,
    sem_cr,
    sem_xs,
    sem_xr,
    sem_hz,
    sem_hy,
    sem_hc,
    sem_hr,
):
    S2, B2, U = S // 2, B // 2, 2 * S
    pairs, width = req_ref.shape
    rows = cold_ref.shape[0]
    hot_rows = hot_ref.shape[0]
    HB = lines_ref.shape[0]
    CB = parent_ref.shape[0]
    RB = rows // B
    HR = hot_rows // U
    s = lax.axis_index("shard")
    b = lax.axis_index("blk")
    line, y = s // 2, lax.rem(s, 2)
    x, c = b // 2, lax.rem(b, 2)
    u = s * 2 + c
    G = 4 if S2 % 4 == 0 else 1

    def place(p, cc):
        return (cc * 2 + lax.rem(p, 2)) * S2 + p // 2

    w = place(s, c)
    ypart = line * 2 + (1 - y)
    cpart = x * 2 + (1 - c)
    dot = functools.partial(lax.dot_general, preferred_element_type=F32)

    def send(src, dst, ss, rs, sh, bl):
        return pltpu.make_async_remote_copy(
            src_ref=src,
            dst_ref=dst,
            send_sem=ss,
            recv_sem=rs,
            device_id=(sh, bl),
            device_id_type=pl.DeviceIdType.MESH,
        )

    def loop(lo, hi, f):
        def body(i, carry):
            f(i)
            return carry

        lax.fori_loop(lo, hi, body, 0)

    barrier = pltpu.get_barrier_semaphore()

    def greet(k):
        v = lax.rem(u + k, U)
        pl.semaphore_signal(
            barrier,
            inc=1,
            device_id=(v // 2, x * 2 + lax.rem(v, 2)),
            device_id_type=pl.DeviceIdType.MESH,
        )

    loop(1, U, greet)

    def greet_blk(k):
        xo = lax.rem(x + k, B2)
        for cc in range(2):
            pl.semaphore_signal(
                barrier, inc=1, device_id=(s, xo * 2 + cc), device_id_type=pl.DeviceIdType.MESH
            )

    loop(1, B2, greet_blk)

    slot = lax.broadcasted_iota(jnp.int32, (CB, pairs), 0)
    cold_key = jnp.where(slot < tally_ref[...], parent_ref[...] * rows + pos_ref[...], -1)
    keys[w] = jnp.concatenate([lines_ref[...], cold_key], axis=0)

    qf = req_ref[...].astype(F32)
    q_unit, q_radius = normalize_rows(qf)
    qunit[...] = q_unit
    queries[b] = q_unit.astype(BF)

    pl.semaphore_wait(barrier, U - 1 + 2 * (B2 - 1))

    def key_copy(src_w, k, p, cc):
        return send(keys.at[src_w], keys.at[src_w], sem_ks.at[k], sem_kr.at[src_w], p, x * 2 + cc)

    def send_keys(k):
        key_copy(w, k, lax.rem(s + k, S), c).start()

    def send_keys_core(k):
        key_copy(w, S + k, lax.rem(s + k, S), 1 - c).start()

    loop(1, S, send_keys)
    loop(0, S, send_keys_core)

    def q_copy(slot_b, k, bo):
        return send(
            queries.at[slot_b], queries.at[slot_b], sem_qs.at[k], sem_qr.at[slot_b], s, bo
        )

    loop(1, B, lambda k: q_copy(b, k, lax.rem(b + k, B)).start())

    coldb[...] = cold_ref[...].astype(BF)

    def one_hot(where, idx):
        same = where.astype(jnp.int16) == idx.astype(jnp.int16)
        return jnp.where(same, jnp.ones((), BF), jnp.zeros((), BF))

    def own_index(block):
        rel = block[HB : HB + CB, :] - s * rows
        good = (rel >= 0) & (rel < rows) & (block[HB : HB + CB, :] >= 0)
        return jnp.max(jnp.where(good, rel, -1), axis=0, keepdims=True)

    def lookup(p):
        idx = own_index(keys[place(p, c)])
        col = jnp.transpose(jnp.broadcast_to(idx, (128, pairs)))[:, :1]
        hit = one_hot(lax.broadcasted_iota(jnp.int32, (pairs, rows), 1), col)
        return dot(hit, coldb[...], (((1,), (0,)), ((), ())))

    def y_copy(lo):
        return send(ysend.at[lo], yrecv.at[lo], sem_ys.at[lo], sem_yr.at[lo], ypart, b)

    def z_copy(src, dst, lo):
        return send(zsend.at[src], zrecv.at[dst], sem_zs.at[src], sem_zr.at[dst], lo * 2 + y, b)

    def wait_key(p, cc):
        key_copy(place(p, cc), 0, p, cc).wait_recv()

    def fetch_y(k):
        lo = lax.rem(line + k, S2)
        p = lo * 2 + (1 - y)
        wait_key(p, c)
        ysend[lo] = lookup(p).astype(BF)
        y_copy(lo).start()

    loop(1, S2 + 1, fetch_y)

    def fetch_z(k):
        lo = lax.rem(line + k, S2)
        p = lo * 2 + y
        wait_key(p, c)
        part = lookup(p)
        y_copy(lo).wait_recv()
        zsend[lo] = (part + yrecv[lo].astype(F32)).astype(BF)
        z_copy(lo, line, lo).start()

    loop(1, S2, fetch_z)

    own_keys = jnp.concatenate([keys[w]] * (128 // (HB + CB)), axis=0)
    lines = jnp.transpose(own_keys)
    hot_iota = lax.broadcasted_iota(jnp.int32, (pairs, hot_rows), 1)
    counts = jnp.zeros((pairs, hot_rows), BF)
    for h in range(HB):
        counts = counts + one_hot(hot_iota, lines[:, h : h + 1])
    item = dot(counts, hot_ref[...], (((1,), (0,)), ((), ())))
    item = item + lookup(s)
    y_copy(line).wait_recv()
    item = item + yrecv[line].astype(F32)

    def take_z(k, acc):
        lo = lax.rem(line + S2 - k, S2)
        z_copy(line, lo, lo).wait_recv()
        return acc + zrecv[lo].astype(F32)

    item = lax.fori_loop(1, S2, take_z, item)

    unit, radius = normalize_rows(item)
    low = unit.astype(BF)
    scale = scale_ref[0]
    bias = bias_ref[0]
    diag = lax.broadcasted_iota(jnp.int32, (pairs, pairs), 0) == lax.broadcasted_iota(
        jnp.int32, (pairs, pairs), 1
    )

    def pair_grads(q, positive):
        logits = scale * dot(low, q, (((1,), (1,)), ((), ()))) + bias
        g = jax.nn.sigmoid(logits)
        if positive:
            g = g - diag.astype(F32)
        g = g.astype(BF)
        return dot(g, q, (((1,), (0,)), ((), ()))), dot(g, low, (((0,), (0,)), ((), ())))

    item_dir, own_qdir = pair_grads(queries[b], True)
    qdir[...] = own_qdir

    def p_copy(bo, dst):
        return send(qsend.at[bo], qrecv.at[dst], sem_ps.at[bo], sem_pr.at[dst], s, bo)

    def loss_block(k, acc):
        bo = lax.rem(b + k, B)
        q_copy(bo, 0, bo).wait_recv()
        add, part = pair_grads(queries[bo], False)
        qsend[bo] = part.astype(BF)
        p_copy(bo, b).start()
        return acc + add

    item_dir = lax.fori_loop(1, B, loss_block, item_dir)
    grads[w] = projection_backward(unit, radius, scale * item_dir).astype(BF)

    def gz_copy(v, lo, way):
        return send(
            grads.at[v],
            grads.at[v],
            sem_gz.at[(way + 1) // 2 * S2 + lo],
            sem_gr.at[v],
            (line + way) * 2 + y,
            b,
        )

    def gy_copy(v, lo):
        return send(grads.at[v], grads.at[v], sem_gy.at[lo], sem_gr.at[v], ypart, b)

    def gc_copy(v, p):
        return send(grads.at[v], grads.at[v], sem_gc.at[p], sem_gr.at[v], s, cpart)

    def hop(copy, lo, v, way, act):
        ahead = line + way

        @pl.when((ahead >= 0) & (ahead < S2))
        def _():
            act(copy(v, lo, way))

    def from_line(wait, d):
        for way in (1, -1):
            lo = line - way * d

            @pl.when((lo >= 0) & (lo < S2))
            def _():
                wait(lo, way)

    def sent_hops(copy, block_of):
        def right(lo):
            @pl.when((lo <= line) & (line + 1 < S2))
            def _():
                copy(block_of(lo), lo, 1).wait_send()

        def left(lo):
            @pl.when((lo >= line) & (line > 0))
            def _():
                copy(block_of(lo), lo, -1).wait_send()

        loop(0, S2, right)
        loop(0, S2, left)

    for way in (1, -1):
        hop(gz_copy, line, w, way, lambda d: d.start())
    gy_copy(w, line).start()
    gc_copy(w, s).start()

    coldacc[...] = jnp.zeros(coldacc.shape, F32)
    hotacc[...] = jnp.zeros(hotacc.shape, F32)
    row_iota = lax.broadcasted_iota(jnp.int32, (RB, G * pairs), 0)
    hrow_iota = lax.broadcasted_iota(jnp.int32, (HR, G * pairs), 0)

    def group_rows(first):
        return jnp.concatenate([grads[first + i] for i in range(G)], axis=0)

    def add_hot(group):
        def chunk(i):
            first = group * S2 + i * G
            ids = jnp.concatenate([keys[first + j][:HB, :] for j in range(G)], axis=1) - u * HR
            ids = jnp.where((ids >= 0) & (ids < HR), ids, -1)
            cnt = jnp.zeros((HR, G * pairs), BF)
            for h in range(HB):
                cnt = cnt + one_hot(hrow_iota, ids[h : h + 1, :])
            hotacc[...] += dot(cnt, group_rows(first), (((1,), (0,)), ((), ())))

        loop(0, S2 // G, chunk)

    def add_cold(group, xo):
        def chunk(i):
            first = group * S2 + i * G
            ids = jnp.concatenate([own_index(keys[first + j]) for j in range(G)], axis=1)
            hit = one_hot(row_iota, ids - (xo * 2 + c) * RB)
            coldacc[xo] += dot(hit, group_rows(first), (((1,), (0,)), ((), ())))

        loop(0, S2 // G, chunk)

    def line_column(lo, way):
        p = lo * 2 + y
        v = place(p, c)
        gz_copy(v, lo, -way).wait_recv()
        hop(gz_copy, lo, v, way, lambda d: d.start())
        gy_copy(v, lo).start()
        gc_copy(v, p).start()

    loop(1, S2, functools.partial(from_line, line_column))
    mine, other = c * 2, (1 - c) * 2
    add_hot(mine + y)
    loop(0, B2, lambda xo: add_cold(mine + y, xo))

    def y_column(k):
        lo = lax.rem(line + S2 - k, S2)
        p = lo * 2 + (1 - y)
        v = place(p, c)
        gy_copy(v, lo).wait_recv()
        gc_copy(v, p).start()

    loop(0, S2, y_column)

    def core_column(yy):
        def one(k):
            p = lax.rem(line + S2 - k, S2) * 2 + yy
            wait_key(p, 1 - c)
            gc_copy(place(p, 1 - c), p).wait_recv()

        loop(0, S2, one)

    core_column(y)
    for group in (other + y, mine + 1 - y):
        add_hot(group)
        loop(0, B2, functools.partial(add_cold, group))
    core_column(1 - y)
    last = other + 1 - y
    add_hot(last)

    def x_copy(dst, xo):
        return send(
            hpart.at[x], hpart.at[dst], sem_xs.at[xo], sem_xr.at[dst], s, xo * 2 + c
        )

    hpart[x] = hotacc[...].astype(BF)
    loop(1, B2, lambda k: x_copy(x, lax.rem(x + k, B2)).start())

    def c_copy(src, dst):
        return send(
            csend.at[src], crecv.at[dst], sem_cs.at[src], sem_cr.at[dst], s, src * 2 + c
        )

    def send_cold(k):
        xo = lax.rem(x + k, B2)
        add_cold(last, xo)
        csend[xo] = coldacc[xo].astype(BF)
        c_copy(xo, x).start()

    loop(1, B2, send_cold)

    def wait_x(k):
        xo = lax.rem(x + k, B2)
        x_copy(xo, xo).wait_recv()

    loop(1, B2, wait_x)
    total = hpart[0].astype(F32)
    for xo in range(1, B2):
        total = total + hpart[xo].astype(F32)
    hfull[u] = total.astype(BF)

    def hz_copy(v, lo, way):
        return send(
            hfull.at[v],
            hfull.at[v],
            sem_hz.at[(way + 1) // 2 * S2 + lo],
            sem_hr.at[v],
            (line + way) * 2 + y,
            b,
        )

    def hy_copy(v, lo):
        return send(hfull.at[v], hfull.at[v], sem_hy.at[lo], sem_hr.at[v], ypart, b)

    def hc_copy(v, p):
        return send(hfull.at[v], hfull.at[v], sem_hc.at[p], sem_hr.at[v], s, cpart)

    for way in (1, -1):
        hop(hz_copy, line, u, way, lambda d: d.start())
    hy_copy(u, line).start()
    hc_copy(u, s).start()

    def hot_line(lo, way):
        p = lo * 2 + y
        v = p * 2 + c
        hz_copy(v, lo, -way).wait_recv()
        hop(hz_copy, lo, v, way, lambda d: d.start())
        hy_copy(v, lo).start()
        hc_copy(v, p).start()

    loop(1, S2, functools.partial(from_line, hot_line))

    def hot_y(k):
        lo = lax.rem(line + S2 - k, S2)
        p = lo * 2 + (1 - y)
        v = p * 2 + c
        hy_copy(v, lo).wait_recv()
        hc_copy(v, p).start()

    loop(0, S2, hot_y)

    add_cold(last, x)

    def take_p(k, acc):
        bo = lax.rem(b + k, B)
        p_copy(bo, bo).wait_recv()
        return acc + qrecv[bo].astype(F32)

    q_total = lax.fori_loop(1, B, take_p, qdir[...])
    _, q_radius2 = normalize_rows(req_ref[...].astype(F32))
    dq_ref[...] = projection_backward(qunit[...], q_radius2, scale * q_total)

    def take_cold(k, acc):
        xo = lax.rem(x + k, B2)
        c_copy(xo, xo).wait_recv()
        return acc + crecv[xo].astype(F32)

    coldg_ref[...] = lax.fori_loop(1, B2, take_cold, coldacc[x])

    def hot_core(k):
        p = lax.rem(s + S - k, S)
        hc_copy(p * 2 + (1 - c), p).wait_recv()

    loop(0, S, hot_core)
    hotg_ref[...] = hfull[...]

    loop(1, S, lambda k: key_copy(w, k, lax.rem(s + k, S), c).wait_send())
    loop(0, S, lambda k: key_copy(w, S + k, lax.rem(s + k, S), 1 - c).wait_send())
    loop(1, B, lambda k: q_copy(b, k, lax.rem(b + k, B)).wait_send())
    loop(0, S2, lambda lo: y_copy(lo).wait_send())

    def sent_line(k):
        lo = lax.rem(line + k, S2)
        z_copy(lo, line, lo).wait_send()

    loop(1, S2, sent_line)
    sent_hops(gz_copy, lambda lo: place(lo * 2 + y, c))
    sent_hops(hz_copy, lambda lo: (lo * 2 + y) * 2 + c)
    loop(1, B, lambda k: p_copy(lax.rem(b + k, B), b).wait_send())

    def sent_y(lo):
        gy_copy(place(lo * 2 + y, c), lo).wait_send()
        hy_copy((lo * 2 + y) * 2 + c, lo).wait_send()

    loop(0, S2, sent_y)

    def sent_c(p):
        gc_copy(place(p, c), p).wait_send()
        hc_copy(p * 2 + c, p).wait_send()

    loop(0, S, sent_c)

    def sent_x(k):
        xo = lax.rem(x + k, B2)
        x_copy(x, xo).wait_send()
        c_copy(xo, x).wait_send()

    loop(1, B2, sent_x)


def body(
    request_embeddings,
    frequent_entry_matrix,
    rare_entry_matrix,
    frequent_entry_lines,
    rare_place_parent,
    rare_local_position,
    rare_place_tally,
    sharpness_factor,
    pairscore_additive,
):
    pairs, width = request_embeddings.shape
    S = lax.axis_size("shard")
    B = lax.axis_size("blk")
    rows = rare_entry_matrix.shape[0]
    hot_rows = frequent_entry_matrix.shape[0]
    S2, B2, U = S // 2, B // 2, 2 * S
    RB, HR = rows // B, hot_rows // U
    ids = frequent_entry_lines.shape[1] + rare_place_parent.shape[1]
    vmem = pl.BlockSpec(memory_space=pltpu.VMEM)
    smem = pl.BlockSpec(memory_space=pltpu.SMEM)
    dma = lambda n: pltpu.SemaphoreType.DMA((n,))
    blocks = lambda n, dtype: pltpu.VMEM((n, pairs, width), dtype)
    dq, hot, cold = pl.pallas_call(
        functools.partial(kernel, S, B),
        out_shape=(
            jax.ShapeDtypeStruct((pairs, width), F32),
            jax.ShapeDtypeStruct((U, HR, width), BF),
            jax.ShapeDtypeStruct((RB, width), F32),
        ),
        in_specs=[smem, smem] + [vmem] * 7,
        out_specs=(vmem, vmem, vmem),
        scratch_shapes=[
            pltpu.VMEM((U, ids, pairs), jnp.int32),
            pltpu.VMEM((rows, width), BF),
            blocks(S2, BF),
            blocks(S2, BF),
            blocks(S2, BF),
            blocks(S2, BF),
            blocks(B, BF),
            blocks(B, BF),
            blocks(B, BF),
            pltpu.VMEM((pairs, width), F32),
            pltpu.VMEM((pairs, width), F32),
            blocks(U, BF),
            pltpu.VMEM((B2, RB, width), F32),
            pltpu.VMEM((B2, RB, width), BF),
            pltpu.VMEM((B2, RB, width), BF),
            pltpu.VMEM((HR, width), F32),
            pltpu.VMEM((B2, HR, width), BF),
            pltpu.VMEM((U, HR, width), BF),
            dma(U),
            dma(U),
            dma(S2),
            dma(S2),
            dma(S2),
            dma(S2),
            dma(B),
            dma(B),
            dma(B),
            dma(B),
            dma(2 * S2),
            dma(S2),
            dma(S),
            dma(U),
            dma(B2),
            dma(B2),
            dma(B2),
            dma(B2),
            dma(2 * S2),
            dma(S2),
            dma(S),
            dma(U),
        ],
        compiler_params=pltpu.CompilerParams(
            collective_id=0, has_side_effects=True, vmem_limit_bytes=56 * 1024 * 1024
        ),
    )(
        sharpness_factor,
        pairscore_additive,
        request_embeddings,
        frequent_entry_matrix,
        rare_entry_matrix,
        frequent_entry_lines.T,
        rare_place_parent.T,
        rare_local_position.T,
        rare_place_tally.reshape(1, pairs),
    )
    return dq, hot.reshape(hot_rows, width).astype(F32), cold


def solution(mesh):
    in_specs = (
        P(("shard", "blk"), None),
        P(),
        P("shard", None),
        P(("shard", "blk"), None),
        P(("shard", "blk"), None),
        P(("shard", "blk"), None),
        P(("shard", "blk")),
        P(),
        P(),
    )
    out_specs = (P(("shard", "blk"), None), P(), P(("shard", "blk"), None))
    return jax.shard_map(body, mesh=mesh, in_specs=in_specs, out_specs=out_specs, check_vma=False)
```

```python
import functools

import jax
import jax.numpy as jnp
from jax import lax
from jax.experimental import pallas as pl
from jax.experimental.pallas import tpu as pltpu
from jax.sharding import PartitionSpec as P

epsilon = 1e-06
BF = jnp.bfloat16
F32 = jnp.float32


def normalize_rows(vectors):
    radius = jnp.sqrt(jnp.sum(vectors * vectors, axis=1, keepdims=True) + epsilon)
    return (vectors / radius, radius)


def projection_backward(unit_vectors, radius, gradient):
    inner = jnp.sum(unit_vectors * gradient, axis=1, keepdims=True)
    return (gradient - unit_vectors * inner) / radius


def kernel(
    S,
    B,
    scale_ref,
    bias_ref,
    req_ref,
    hot_ref,
    cold_ref,
    lines_ref,
    parent_ref,
    pos_ref,
    tally_ref,
    dq_ref,
    hotg_ref,
    coldg_ref,
    keys,
    coldb,
    ysend,
    yrecv,
    zsend,
    zrecv,
    queries,
    qsend,
    qrecv,
    qunit,
    qdir,
    grads,
    coldacc,
    csend,
    crecv,
    hotacc,
    hpart,
    hfull,
    sem_ks,
    sem_kr,
    sem_ys,
    sem_yr,
    sem_zs,
    sem_zr,
    sem_qs,
    sem_qr,
    sem_ps,
    sem_pr,
    sem_gz,
    sem_gy,
    sem_gc,
    sem_gr,
    sem_cs,
    sem_cr,
    sem_xs,
    sem_xr,
    sem_hz,
    sem_hy,
    sem_hc,
    sem_hr,
):
    S2, B2, U = S // 2, B // 2, 2 * S
    pairs, width = req_ref.shape
    rows = cold_ref.shape[0]
    hot_rows = hot_ref.shape[0]
    HB = lines_ref.shape[0]
    CB = parent_ref.shape[0]
    RB = rows // B
    HR = hot_rows // U
    s = lax.axis_index("shard")
    b = lax.axis_index("blk")
    line, y = s // 2, lax.rem(s, 2)
    x, c = b // 2, lax.rem(b, 2)
    u = s * 2 + c
    G = 4 if S2 % 4 == 0 else 1

    def place(p, cc):
        return (cc * 2 + lax.rem(p, 2)) * S2 + p // 2

    w = place(s, c)
    ypart = line * 2 + (1 - y)
    cpart = x * 2 + (1 - c)
    dot = functools.partial(lax.dot_general, preferred_element_type=F32)

    def send(src, dst, ss, rs, sh, bl):
        return pltpu.make_async_remote_copy(
            src_ref=src,
            dst_ref=dst,
            send_sem=ss,
            recv_sem=rs,
            device_id=(sh, bl),
            device_id_type=pl.DeviceIdType.MESH,
        )

    def loop(lo, hi, f):
        def body(i, carry):
            f(i)
            return carry

        lax.fori_loop(lo, hi, body, 0)

    barrier = pltpu.get_barrier_semaphore()

    def greet(k):
        v = lax.rem(u + k, U)
        pl.semaphore_signal(
            barrier,
            inc=1,
            device_id=(v // 2, x * 2 + lax.rem(v, 2)),
            device_id_type=pl.DeviceIdType.MESH,
        )

    loop(1, U, greet)

    def greet_blk(k):
        xo = lax.rem(x + k, B2)
        for cc in range(2):
            pl.semaphore_signal(
                barrier, inc=1, device_id=(s, xo * 2 + cc), device_id_type=pl.DeviceIdType.MESH
            )

    loop(1, B2, greet_blk)

    slot = lax.broadcasted_iota(jnp.int32, (CB, pairs), 0)
    cold_key = jnp.where(slot < tally_ref[...], parent_ref[...] * rows + pos_ref[...], -1)
    keys[w] = jnp.concatenate([lines_ref[...], cold_key], axis=0)

    qf = req_ref[...].astype(F32)
    q_unit, q_radius = normalize_rows(qf)
    qunit[...] = q_unit
    queries[b] = q_unit.astype(BF)

    pl.semaphore_wait(barrier, U - 1 + 2 * (B2 - 1))

    def key_copy(src_w, k, p, cc):
        return send(keys.at[src_w], keys.at[src_w], sem_ks.at[k], sem_kr.at[src_w], p, x * 2 + cc)

    def send_keys(k):
        key_copy(w, k, lax.rem(s + k, S), c).start()

    def send_keys_core(k):
        key_copy(w, S + k, lax.rem(s + k, S), 1 - c).start()

    loop(1, S, send_keys)
    loop(0, S, send_keys_core)

    def q_copy(slot_b, k, bo):
        return send(
            queries.at[slot_b], queries.at[slot_b], sem_qs.at[k], sem_qr.at[slot_b], s, bo
        )

    loop(1, B, lambda k: q_copy(b, k, lax.rem(b + k, B)).start())

    coldb[...] = cold_ref[...].astype(BF)

    def one_hot(where, idx):
        same = where.astype(jnp.int16) == idx.astype(jnp.int16)
        return jnp.where(same, jnp.ones((), BF), jnp.zeros((), BF))

    def own_index(block):
        rel = block[HB : HB + CB, :] - s * rows
        good = (rel >= 0) & (rel < rows) & (block[HB : HB + CB, :] >= 0)
        return jnp.max(jnp.where(good, rel, -1), axis=0, keepdims=True)

    def lookup(p):
        idx = own_index(keys[place(p, c)])
        col = jnp.transpose(jnp.broadcast_to(idx, (128, pairs)))[:, :1]
        hit = one_hot(lax.broadcasted_iota(jnp.int32, (pairs, rows), 1), col)
        return dot(hit, coldb[...], (((1,), (0,)), ((), ())))

    def y_copy(lo):
        return send(ysend.at[lo], yrecv.at[lo], sem_ys.at[lo], sem_yr.at[lo], ypart, b)

    def z_copy(src, dst, lo):
        return send(zsend.at[src], zrecv.at[dst], sem_zs.at[src], sem_zr.at[dst], lo * 2 + y, b)

    def wait_key(p, cc):
        key_copy(place(p, cc), 0, p, cc).wait_recv()

    def fetch_y(k):
        lo = lax.rem(line + k, S2)
        p = lo * 2 + (1 - y)
        wait_key(p, c)
        ysend[lo] = lookup(p).astype(BF)
        y_copy(lo).start()

    loop(1, S2 + 1, fetch_y)

    def fetch_z(k):
        lo = lax.rem(line + k, S2)
        p = lo * 2 + y
        wait_key(p, c)
        part = lookup(p)
        y_copy(lo).wait_recv()
        zsend[lo] = (part + yrecv[lo].astype(F32)).astype(BF)
        z_copy(lo, line, lo).start()

    loop(1, S2, fetch_z)

    own_keys = jnp.concatenate([keys[w]] * (128 // (HB + CB)), axis=0)
    lines = jnp.transpose(own_keys)
    hot_iota = lax.broadcasted_iota(jnp.int32, (pairs, hot_rows), 1)
    counts = jnp.zeros((pairs, hot_rows), BF)
    for h in range(HB):
        counts = counts + one_hot(hot_iota, lines[:, h : h + 1])
    item = dot(counts, hot_ref[...], (((1,), (0,)), ((), ())))
    item = item + lookup(s)
    y_copy(line).wait_recv()
    item = item + yrecv[line].astype(F32)

    def take_z(k, acc):
        lo = lax.rem(line + S2 - k, S2)
        z_copy(line, lo, lo).wait_recv()
        return acc + zrecv[lo].astype(F32)

    item = lax.fori_loop(1, S2, take_z, item)

    unit, radius = normalize_rows(item)
    low = unit.astype(BF)
    scale = scale_ref[0]
    bias = bias_ref[0]
    diag = lax.broadcasted_iota(jnp.int32, (pairs, pairs), 0) == lax.broadcasted_iota(
        jnp.int32, (pairs, pairs), 1
    )

    def pair_grads(q, positive):
        logits = scale * dot(low, q, (((1,), (1,)), ((), ()))) + bias
        g = jax.nn.sigmoid(logits)
        if positive:
            g = g - diag.astype(F32)
        g = g.astype(BF)
        return dot(g, q, (((1,), (0,)), ((), ()))), dot(g, low, (((0,), (0,)), ((), ())))

    item_dir, own_qdir = pair_grads(queries[b], True)
    qdir[...] = own_qdir

    def p_copy(bo, dst):
        return send(qsend.at[bo], qrecv.at[dst], sem_ps.at[bo], sem_pr.at[dst], s, bo)

    def loss_block(k, acc):
        bo = lax.rem(b + k, B)
        q_copy(bo, 0, bo).wait_recv()
        add, part = pair_grads(queries[bo], False)
        qsend[bo] = part.astype(BF)
        p_copy(bo, b).start()
        return acc + add

    item_dir = lax.fori_loop(1, B, loss_block, item_dir)
    grads[w] = projection_backward(unit, radius, scale * item_dir).astype(BF)

    def gz_copy(v, lo):
        return send(grads.at[v], grads.at[v], sem_gz.at[lo], sem_gr.at[v], lo * 2 + y, b)

    def gy_copy(v, lo):
        return send(grads.at[v], grads.at[v], sem_gy.at[lo], sem_gr.at[v], ypart, b)

    def gc_copy(v, p):
        return send(grads.at[v], grads.at[v], sem_gc.at[p], sem_gr.at[v], s, cpart)

    loop(1, S2, lambda k: gz_copy(w, lax.rem(line + k, S2)).start())
    gy_copy(w, line).start()
    gc_copy(w, s).start()

    coldacc[...] = jnp.zeros(coldacc.shape, F32)
    hotacc[...] = jnp.zeros(hotacc.shape, F32)
    row_iota = lax.broadcasted_iota(jnp.int32, (RB, G * pairs), 0)
    hrow_iota = lax.broadcasted_iota(jnp.int32, (HR, G * pairs), 0)

    def group_rows(first):
        return jnp.concatenate([grads[first + i] for i in range(G)], axis=0)

    def add_hot(group):
        def chunk(i):
            first = group * S2 + i * G
            ids = jnp.concatenate([keys[first + j][:HB, :] for j in range(G)], axis=1) - u * HR
            ids = jnp.where((ids >= 0) & (ids < HR), ids, -1)
            cnt = jnp.zeros((HR, G * pairs), BF)
            for h in range(HB):
                cnt = cnt + one_hot(hrow_iota, ids[h : h + 1, :])
            hotacc[...] += dot(cnt, group_rows(first), (((1,), (0,)), ((), ())))

        loop(0, S2 // G, chunk)

    def add_cold(group, xo):
        def chunk(i):
            first = group * S2 + i * G
            ids = jnp.concatenate([own_index(keys[first + j]) for j in range(G)], axis=1)
            hit = one_hot(row_iota, ids - (xo * 2 + c) * RB)
            coldacc[xo] += dot(hit, group_rows(first), (((1,), (0,)), ((), ())))

        loop(0, S2 // G, chunk)

    def line_column(k):
        lo = lax.rem(line + S2 - k, S2)
        p = lo * 2 + y
        v = place(p, c)
        gz_copy(v, lo).wait_recv()
        gy_copy(v, lo).start()
        gc_copy(v, p).start()

    loop(1, S2, line_column)
    mine, other = c * 2, (1 - c) * 2
    add_hot(mine + y)
    loop(0, B2, lambda xo: add_cold(mine + y, xo))

    def y_column(k):
        lo = lax.rem(line + S2 - k, S2)
        p = lo * 2 + (1 - y)
        v = place(p, c)
        gy_copy(v, lo).wait_recv()
        gc_copy(v, p).start()

    loop(0, S2, y_column)

    def core_column(yy):
        def one(k):
            p = lax.rem(line + S2 - k, S2) * 2 + yy
            wait_key(p, 1 - c)
            gc_copy(place(p, 1 - c), p).wait_recv()

        loop(0, S2, one)

    core_column(y)
    for group in (other + y, mine + 1 - y):
        add_hot(group)
        loop(0, B2, functools.partial(add_cold, group))
    core_column(1 - y)
    last = other + 1 - y
    add_hot(last)

    def x_copy(dst, xo):
        return send(
            hpart.at[x], hpart.at[dst], sem_xs.at[xo], sem_xr.at[dst], s, xo * 2 + c
        )

    hpart[x] = hotacc[...].astype(BF)
    loop(1, B2, lambda k: x_copy(x, lax.rem(x + k, B2)).start())

    def c_copy(src, dst):
        return send(
            csend.at[src], crecv.at[dst], sem_cs.at[src], sem_cr.at[dst], s, src * 2 + c
        )

    def send_cold(k):
        xo = lax.rem(x + k, B2)
        add_cold(last, xo)
        csend[xo] = coldacc[xo].astype(BF)
        c_copy(xo, x).start()

    loop(1, B2, send_cold)

    def wait_x(k):
        xo = lax.rem(x + k, B2)
        x_copy(xo, xo).wait_recv()

    loop(1, B2, wait_x)
    total = hpart[0].astype(F32)
    for xo in range(1, B2):
        total = total + hpart[xo].astype(F32)
    hfull[u] = total.astype(BF)

    def hz_copy(v, lo):
        return send(hfull.at[v], hfull.at[v], sem_hz.at[lo], sem_hr.at[v], lo * 2 + y, b)

    def hy_copy(v, lo):
        return send(hfull.at[v], hfull.at[v], sem_hy.at[lo], sem_hr.at[v], ypart, b)

    def hc_copy(v, p):
        return send(hfull.at[v], hfull.at[v], sem_hc.at[p], sem_hr.at[v], s, cpart)

    loop(1, S2, lambda k: hz_copy(u, lax.rem(line + k, S2)).start())
    hy_copy(u, line).start()
    hc_copy(u, s).start()

    add_cold(last, x)

    def take_p(k, acc):
        bo = lax.rem(b + k, B)
        p_copy(bo, bo).wait_recv()
        return acc + qrecv[bo].astype(F32)

    q_total = lax.fori_loop(1, B, take_p, qdir[...])
    _, q_radius2 = normalize_rows(req_ref[...].astype(F32))
    dq_ref[...] = projection_backward(qunit[...], q_radius2, scale * q_total)

    def hot_line(k):
        lo = lax.rem(line + S2 - k, S2)
        p = lo * 2 + y
        v = p * 2 + c
        hz_copy(v, lo).wait_recv()
        hy_copy(v, lo).start()
        hc_copy(v, p).start()

    loop(1, S2, hot_line)

    def hot_y(k):
        lo = lax.rem(line + S2 - k, S2)
        p = lo * 2 + (1 - y)
        v = p * 2 + c
        hy_copy(v, lo).wait_recv()
        hc_copy(v, p).start()

    loop(0, S2, hot_y)

    def take_cold(k, acc):
        xo = lax.rem(x + k, B2)
        c_copy(xo, xo).wait_recv()
        return acc + crecv[xo].astype(F32)

    coldg_ref[...] = lax.fori_loop(1, B2, take_cold, coldacc[x])

    def hot_core(k):
        p = lax.rem(s + S - k, S)
        hc_copy(p * 2 + (1 - c), p).wait_recv()

    loop(0, S, hot_core)
    hotg_ref[...] = hfull[...]

    loop(1, S, lambda k: key_copy(w, k, lax.rem(s + k, S), c).wait_send())
    loop(0, S, lambda k: key_copy(w, S + k, lax.rem(s + k, S), 1 - c).wait_send())
    loop(1, B, lambda k: q_copy(b, k, lax.rem(b + k, B)).wait_send())
    loop(0, S2, lambda lo: y_copy(lo).wait_send())

    def sent_line(k):
        lo = lax.rem(line + k, S2)
        z_copy(lo, line, lo).wait_send()
        gz_copy(w, lo).wait_send()
        hz_copy(u, lo).wait_send()

    loop(1, S2, sent_line)
    loop(1, B, lambda k: p_copy(lax.rem(b + k, B), b).wait_send())

    def sent_y(lo):
        gy_copy(place(lo * 2 + y, c), lo).wait_send()
        hy_copy((lo * 2 + y) * 2 + c, lo).wait_send()

    loop(0, S2, sent_y)

    def sent_c(p):
        gc_copy(place(p, c), p).wait_send()
        hc_copy(p * 2 + c, p).wait_send()

    loop(0, S, sent_c)

    def sent_x(k):
        xo = lax.rem(x + k, B2)
        x_copy(x, xo).wait_send()
        c_copy(xo, x).wait_send()

    loop(1, B2, sent_x)


def body(
    request_embeddings,
    frequent_entry_matrix,
    rare_entry_matrix,
    frequent_entry_lines,
    rare_place_parent,
    rare_local_position,
    rare_place_tally,
    sharpness_factor,
    pairscore_additive,
):
    pairs, width = request_embeddings.shape
    S = lax.axis_size("shard")
    B = lax.axis_size("blk")
    rows = rare_entry_matrix.shape[0]
    hot_rows = frequent_entry_matrix.shape[0]
    S2, B2, U = S // 2, B // 2, 2 * S
    RB, HR = rows // B, hot_rows // U
    ids = frequent_entry_lines.shape[1] + rare_place_parent.shape[1]
    vmem = pl.BlockSpec(memory_space=pltpu.VMEM)
    smem = pl.BlockSpec(memory_space=pltpu.SMEM)
    dma = lambda n: pltpu.SemaphoreType.DMA((n,))
    blocks = lambda n, dtype: pltpu.VMEM((n, pairs, width), dtype)
    dq, hot, cold = pl.pallas_call(
        functools.partial(kernel, S, B),
        out_shape=(
            jax.ShapeDtypeStruct((pairs, width), F32),
            jax.ShapeDtypeStruct((U, HR, width), BF),
            jax.ShapeDtypeStruct((RB, width), F32),
        ),
        in_specs=[smem, smem] + [vmem] * 7,
        out_specs=(vmem, vmem, vmem),
        scratch_shapes=[
            pltpu.VMEM((U, ids, pairs), jnp.int32),
            pltpu.VMEM((rows, width), BF),
            blocks(S2, BF),
            blocks(S2, BF),
            blocks(S2, BF),
            blocks(S2, BF),
            blocks(B, BF),
            blocks(B, BF),
            blocks(B, BF),
            pltpu.VMEM((pairs, width), F32),
            pltpu.VMEM((pairs, width), F32),
            blocks(U, BF),
            pltpu.VMEM((B2, RB, width), F32),
            pltpu.VMEM((B2, RB, width), BF),
            pltpu.VMEM((B2, RB, width), BF),
            pltpu.VMEM((HR, width), F32),
            pltpu.VMEM((B2, HR, width), BF),
            pltpu.VMEM((U, HR, width), BF),
            dma(U),
            dma(U),
            dma(S2),
            dma(S2),
            dma(S2),
            dma(S2),
            dma(B),
            dma(B),
            dma(B),
            dma(B),
            dma(S2),
            dma(S2),
            dma(S),
            dma(U),
            dma(B2),
            dma(B2),
            dma(B2),
            dma(B2),
            dma(S2),
            dma(S2),
            dma(S),
            dma(U),
        ],
        compiler_params=pltpu.CompilerParams(
            collective_id=0, has_side_effects=True, vmem_limit_bytes=(20 + 4 * S // 4) * 1024 * 1024
        ),
    )(
        sharpness_factor,
        pairscore_additive,
        request_embeddings,
        frequent_entry_matrix,
        rare_entry_matrix,
        frequent_entry_lines.T,
        rare_place_parent.T,
        rare_local_position.T,
        rare_place_tally.reshape(1, pairs),
    )
    return dq, hot.reshape(hot_rows, width).astype(F32), cold


def solution(mesh):
    in_specs = (
        P(("shard", "blk"), None),
        P(),
        P("shard", None),
        P(("shard", "blk"), None),
        P(("shard", "blk"), None),
        P(("shard", "blk"), None),
        P(("shard", "blk")),
        P(),
        P(),
    )
    out_specs = (P(("shard", "blk"), None), P(), P(("shard", "blk"), None))
    return jax.shard_map(body, mesh=mesh, in_specs=in_specs, out_specs=out_specs, check_vma=False)
```
